32 devices in a mesh: chain: 8 (over z, y), head: 4 (over x, core).
Axes of the slice: x: 2, y: 2, z: 4, core: 2. Of those that a mesh axis runs over, the one named last changes fastest.
Arguments:
- signal: bfloat16 [4096, 16384], P(('chain', 'head')), may hold values from -6 to 6
- input_map: bfloat16 [4096, 2048], P(('chain', 'head')), may hold values from -0.375 to 0.375
- output_map: bfloat16 [4096, 2048], P(('chain', 'head')), may hold values from -6 to 6
- step_size: bfloat16 [4096, 256], P(('chain', 'head')), may hold values from 0.000625 to 1.61
- decay_rate: float32 [256], replicated, may hold values from 0.1 to 0.3125
- skip_gain: float32 [256], replicated, may hold values from 0.5 to 1.5
Outputs:
- mixed: bfloat16 [4096, 16384], P(('chain', 'head'))
The draws below stay inside these ranges and needn't reach their ends.
All inputs are finite; a program needn't handle non-finite values.
Results may differ from the reference program's by a relative error of at most 0.0045.
Values may be sent and summed in bfloat16 or wider, within the bound.
A program may use at most 192 MiB of HBM per device.

```python
from functools import partial
import jax
import jax.numpy as jnp
from jax import lax

HEADS = 256
CHANNEL_WIDTH = 64
SSTATE = 256
HEAD_GROUPS = 8
BLOCK = 256
TOKENS = 4096


def slow_heads(key):
    cutoff = 5
    return jax.random.randint(jax.random.fold_in(key, 11), (HEADS,), 0, 10) < cutoff


def head_rates(key):
    slow = slow_heads(key)
    spread = jax.random.uniform(jax.random.fold_in(key, 12), (HEADS,), jnp.float32)
    root_len = TOKENS ** 0.5
    slow_rate = (14.0 + 6.0 * spread) / root_len
    fast_rate = 0.1 + 0.2 * spread
    return (slow, jnp.where(slow, slow_rate, fast_rate).astype(jnp.float32))


def draw_decay_rate(key, part):
    slow, rates = head_rates(key)
    return rates.astype(jnp.float32)


def draw_step_size(key, part):
    slow, rates = head_rates(key)
    root_len = TOKENS ** 0.5
    fast_base = 0.1 + 0.2 * jax.random.uniform(jax.random.fold_in(key, 13), (HEADS,), jnp.float32)
    starting_shift_amount = jnp.where(slow, 0.085 / root_len, fast_base)
    approximate_guess = 0.5 + jax.random.uniform(jax.random.fold_in(key, 14), (TOKENS, HEADS), jnp.float32)
    slot_numbers = jax.random.randint(jax.random.fold_in(key, 15), (2,), 0, TOKENS)
    token_ordinal = jnp.arange(TOKENS)[:, None]
    spike_amounts = jnp.any(token_ordinal == slot_numbers[None, :], axis=1)
    impulse_signals = 1.2 + 0.4 * jax.random.uniform(jax.random.fold_in(key, 16), (TOKENS, HEADS), jnp.float32)
    impulse_signals = jnp.minimum(impulse_signals, 0.4 / rates[None, :])
    return jnp.where(spike_amounts[:, None], impulse_signals, starting_shift_amount[None, :] * approximate_guess).astype(jnp.bfloat16)


def shard_levels(own_key, extent, split, smallest, top_value):
    factor_of, own = 1.0, jax.random.fold_in(own_key, 6)
    for position, blocks in split:
        draws = jnp.exp(jax.random.uniform(jax.random.fold_in(own, position), (blocks,), jnp.float32, smallest / len(split), top_value / len(split)))
        factor_of = factor_of * jnp.repeat(draws, extent[position] // blocks).reshape([-1 if axis == position else 1 for axis in range(len(extent))])
    return factor_of


def centred(stream_key, dims, deviation, reach, split=(), dtype=jnp.bfloat16):
    level = shard_levels(stream_key, dims, split, -0.22, 0.18) if split else 1.0
    result = jax.random.normal(stream_key, dims, jnp.float32) * deviation * level
    return jnp.minimum(jnp.maximum(result, -reach), reach).astype(dtype)


def setup_inputs(seed: int = 0) -> dict:
    arg_keys = jax.random.split(jax.random.key(seed), 7)
    signal = centred(arg_keys[0], (TOKENS, HEADS * CHANNEL_WIDTH), 1.0, 6.0, ((0, 32),))
    input_map = centred(arg_keys[1], (TOKENS, HEAD_GROUPS * SSTATE), (SSTATE ** -0.5), 0.375, ((0, 32),))
    output_map = centred(arg_keys[2], (TOKENS, HEAD_GROUPS * SSTATE), 1.0, 6.0, ((0, 32),))
    step_size = draw_step_size(jax.random.fold_in(arg_keys[6], 71), 0)
    decay_rate = draw_decay_rate(jax.random.fold_in(arg_keys[6], 71), 0)
    skip_gain = jnp.clip(jax.random.uniform(arg_keys[5], (HEADS,), jnp.float32, 0.5, 1.5), 0.5, 1.5)
    return dict(signal=signal, input_map=input_map, output_map=output_map, step_size=step_size, decay_rate=decay_rate, skip_gain=skip_gain)


def block_pass(decay_rate, skip_gain, carry_state, pieces):
    signal_k, input_k, output_k, step_k = pieces
    block_len = signal_k.shape[0]
    group_heads = HEADS // HEAD_GROUPS
    step_rate = step_k.astype(jnp.float32)
    cumul = jnp.cumsum(-decay_rate[None, :] * step_rate, axis=0)
    input_groups = input_k.reshape(block_len, HEAD_GROUPS, SSTATE).astype(jnp.float32)
    output_groups = output_k.reshape(block_len, HEAD_GROUPS, SSTATE).astype(jnp.float32)
    scores = jnp.einsum("tgn,sgn->gts", output_groups, input_groups)
    scores = jnp.repeat(scores, group_heads, axis=0)
    cumul_heads = cumul.T
    causal = jnp.arange(block_len)[:, None] >= jnp.arange(block_len)[None, :]
    differ = jnp.where(causal[None], cumul_heads[:, :, None] - cumul_heads[:, None, :], 0.0)
    weights = jnp.where(causal[None], jnp.exp(differ), 0.0) * scores * step_rate.T[:, None, :]
    weights = lax.optimization_barrier(weights.astype(jnp.bfloat16)).astype(jnp.float32)
    values = signal_k.reshape(block_len, HEADS, CHANNEL_WIDTH).astype(jnp.float32)
    within = jnp.einsum("hts,shp->thp", weights, values)
    rounded = lax.optimization_barrier(carry_state.astype(jnp.bfloat16)).astype(jnp.float32)
    rounded = rounded.reshape(HEAD_GROUPS, group_heads, CHANNEL_WIDTH, SSTATE)
    carried = jnp.einsum("tgn,gjpn->tgjp", output_groups, rounded).reshape(block_len, HEADS, CHANNEL_WIDTH)
    carried = carried * jnp.exp(cumul)[:, :, None]
    mixed_out = (within + carried + skip_gain[None, :, None] * values).astype(jnp.bfloat16)
    to_end = jnp.exp(cumul[-1][None, :] - cumul) * step_rate
    update = lax.optimization_barrier((to_end[:, :, None] * values).astype(jnp.bfloat16)).astype(jnp.float32)
    update = update.reshape(block_len, HEAD_GROUPS, group_heads, CHANNEL_WIDTH)
    fresh_state = jnp.einsum("sgjp,sgn->gjpn", update, input_groups).reshape(HEADS, CHANNEL_WIDTH, SSTATE)
    new_state = jnp.exp(cumul[-1])[:, None, None] * carry_state + fresh_state
    return new_state, mixed_out.reshape(block_len, HEADS * CHANNEL_WIDTH)


def reference(signal, input_map, output_map, step_size, decay_rate, skip_gain):
    blocks = TOKENS // BLOCK
    pieces = (signal.reshape(blocks, BLOCK, HEADS * CHANNEL_WIDTH),
              input_map.reshape(blocks, BLOCK, HEAD_GROUPS * SSTATE),
              output_map.reshape(blocks, BLOCK, HEAD_GROUPS * SSTATE),
              step_size.reshape(blocks, BLOCK, HEADS))
    start_state = jnp.zeros((HEADS, CHANNEL_WIDTH, SSTATE), jnp.float32)
    final_state, result_tensors = lax.scan(partial(block_pass, decay_rate, skip_gain), start_state, pieces)
    return result_tensors.reshape(TOKENS, HEADS * CHANNEL_WIDTH)
```

```python
import functools
import math

import jax
import jax.numpy as jnp
from jax import lax
from jax.experimental import pallas as pl
from jax.experimental.pallas import tpu as pltpu
from jax.sharding import PartitionSpec as P

HEADS = 256
CHANNEL_WIDTH = 64
SSTATE = 256
HEAD_GROUPS = 8
BLOCK = 256
GROUP_HEADS = HEADS // HEAD_GROUPS
PART_HEADS = 4
PART = PART_HEADS * CHANNEL_WIDTH
LOG2E = 1.0 / math.log(2.0)
MESH = pl.DeviceIdType.MESH


def dot(a, b):
    return jnp.dot(a, b, preferred_element_type=jnp.float32)


def kernel(
    head_len, chain_len,
    signal, in_map, out_map, step, rate_row, skip_row, mixed,
    sig_buf, in_buf, out_map_buf, step_buf, u_rows, scores, in_t, cols_ref,
    states, befores, partial_out, grow, out_buf, arriving, leaving,
    meta_local, meta_send, meta_recv, sig_local, sig_send, sig_recv,
    state_send, state_recv, out_local, out_send, out_recv,
):
    me = lax.axis_index("head")
    pos = lax.axis_index("chain")
    rows = signal.shape[0]
    local_heads = HEADS // head_len
    cols = local_heads * CHANNEL_WIDTH
    parts = cols // PART
    groups = max(1, local_heads // GROUP_HEADS)
    map_cols = groups * SSTATE
    blocks = rows * head_len // BLOCK

    def head_peer(r):
        return lax.rem(me + r, head_len)

    barrier = pltpu.get_barrier_semaphore()
    for r in range(1, head_len):
        pl.semaphore_signal(barrier, inc=1, device_id={"head": head_peer(r)}, device_id_type=MESH)
    for d in (1, chain_len - 1):
        pl.semaphore_signal(
            barrier, inc=1, device_id={"chain": lax.rem(pos + d, chain_len)}, device_id_type=MESH
        )

    my_rows = pl.ds(pl.multiple_of(me * rows, rows), rows)

    def map_cols_of(peer):
        start = (peer * local_heads) // GROUP_HEADS * SSTATE
        return pl.ds(pl.multiple_of(start, SSTATE), map_cols)

    def part_cols(j):
        return pl.ds(pl.multiple_of(j * PART, PART), PART)

    def wide_cols(peer, j):
        return pl.ds(pl.multiple_of(peer * cols + j * PART, PART), PART)

    def meta_pairs(peer):
        return (
            (step, step_buf.at[my_rows, :]),
            (in_map.at[:, map_cols_of(peer)], in_buf.at[my_rows, :]),
            (out_map.at[:, map_cols_of(peer)], out_map_buf.at[my_rows, :]),
        )

    def meta_copy(r, i):
        src, dst = meta_pairs(head_peer(r))[i]
        return pltpu.make_async_remote_copy(
            src_ref=src, dst_ref=dst, send_sem=meta_send.at[i, r], recv_sem=meta_recv.at[i, r],
            device_id={"head": head_peer(r)}, device_id_type=MESH,
        )

    def meta_own(i):
        src, dst = meta_pairs(me)[i]
        return pltpu.make_async_copy(src, dst, meta_local.at[i])

    def sig_own():
        src = signal.at[:, pl.ds(pl.multiple_of(me * cols, PART), cols)]
        return pltpu.make_async_copy(src, sig_buf.at[my_rows, :], sig_local)

    def sig_copy(j, r):
        return pltpu.make_async_remote_copy(
            src_ref=signal.at[:, wide_cols(head_peer(r), j)],
            dst_ref=sig_buf.at[my_rows, part_cols(j)],
            send_sem=sig_send.at[j, r], recv_sem=sig_recv.at[j, r],
            device_id={"head": head_peer(r)}, device_id_type=MESH,
        )

    def state_copy(j):
        return pltpu.make_async_remote_copy(
            src_ref=leaving.at[:, part_cols(j)], dst_ref=arriving.at[:, part_cols(j)],
            send_sem=state_send.at[j], recv_sem=state_recv.at[j],
            device_id={"chain": lax.rem(pos + 1, chain_len)}, device_id_type=MESH,
        )

    def out_copy(j, r):
        peer = head_peer(r)
        return pltpu.make_async_remote_copy(
            src_ref=out_buf.at[pl.ds(pl.multiple_of(peer * rows, rows), rows), part_cols(j)],
            dst_ref=mixed.at[:, wide_cols(me, j)],
            send_sem=out_send.at[j, r], recv_sem=out_recv.at[j, r],
            device_id={"head": peer}, device_id_type=MESH,
        )

    def out_own(j):
        return pltpu.make_async_copy(
            out_buf.at[my_rows, part_cols(j)], mixed.at[:, wide_cols(me, j)], out_local.at[j]
        )

    for i in range(3):
        meta_own(i).start()
    sig_own().start()
    pl.semaphore_wait(barrier, head_len + 1)
    for i in range(3):
        for r in range(1, head_len):
            meta_copy(r, i).start()

    def send_signal(j, _):
        for r in range(1, head_len):
            sig_copy(j, r).start()
        return 0

    lax.fori_loop(0, parts, send_signal, 0)

    first = lax.broadcasted_iota(jnp.int32, (BLOCK, BLOCK), 0)
    second = lax.broadcasted_iota(jnp.int32, (BLOCK, BLOCK), 1)
    eye = first == second
    cols_ref[:, 0:1] = jnp.sum(jnp.where(eye, rate_row[...], 0.0), axis=1, keepdims=True)
    cols_ref[:, 1:2] = jnp.sum(jnp.where(eye, skip_row[...], 0.0), axis=1, keepdims=True)

    for i in range(3):
        meta_own(i).wait()
        for r in range(1, head_len):
            meta_copy(r, i).wait_recv()
    sig_own().wait()

    def block_rows(b):
        return pl.ds(pl.multiple_of(b * BLOCK, BLOCK), BLOCK)

    def prepare(b, _):
        until = (first <= second).astype(jnp.float32).astype(jnp.bfloat16)
        step_t = jnp.transpose(step_buf[block_rows(b), :].astype(jnp.float32))
        sums = dot(step_t.astype(jnp.bfloat16), until)
        u_rows[b] = (-cols_ref[:, 0:1] * sums - jnp.log(step_t)) * LOG2E
        for g in range(groups):
            window = slice(g * SSTATE, (g + 1) * SSTATE)
            in_g = in_buf[block_rows(b), window]
            in_gt = jnp.transpose(in_g.astype(jnp.float32)).astype(jnp.bfloat16)
            in_t[b * groups + g] = in_gt
            scores[b * groups + g] = jnp.where(
                first >= second, dot(out_map_buf[block_rows(b), window], in_gt), 0.0
            )
        return 0

    lax.fori_loop(0, blocks, prepare, 0)

    half = BLOCK // 2
    low_lane = lax.broadcasted_iota(jnp.int32, (BLOCK, 128), 1) < CHANNEL_WIDTH
    low_row = lax.broadcasted_iota(jnp.int32, (1, 128), 1) < CHANNEL_WIDTH

    def local_part(j):
        for r in range(1, head_len):
            sig_copy(j, r).wait_recv()
        group = (j * PART_HEADS) // GROUP_HEADS
        head0 = me * local_heads + j * PART_HEADS
        spread = lax.broadcasted_iota(jnp.int32, (HEADS, PART_HEADS * 128), 1) // 128
        chosen = lax.broadcasted_iota(jnp.int32, (HEADS, PART_HEADS * 128), 0) == head0 + spread
        pick = chosen.astype(jnp.float32).astype(jnp.bfloat16)
        slope = jnp.sum(jnp.where(chosen, cols_ref[:, 0:1], 0.0), axis=0, keepdims=True) * -LOG2E
        gains = jnp.sum(jnp.where(chosen, cols_ref[:, 1:2], 0.0), axis=0, keepdims=True)
        lower = (first >= second).astype(jnp.float32).astype(jnp.bfloat16)
        states[0, :, part_cols(j)] = jnp.zeros((SSTATE, PART), jnp.float32)
        befores[0, :, part_cols(j)] = jnp.zeros((8, PART), jnp.float32)

        def one_block(b, _):
            here = block_rows(b)
            wide_step = dot(step_buf[here, :], pick)
            cumul = dot(lower, wide_step.astype(jnp.bfloat16)) * slope
            log_step = jnp.log(wide_step) * LOG2E
            score = b * groups + group
            for q in range(PART_HEADS // 2):
                at = pl.ds(pl.multiple_of(j * PART + q * 128, 128), 128)
                values = sig_buf[here, at]
                wide_values = values.astype(jnp.float32)
                gain = jnp.where(
                    low_row, gains[:, 256 * q:256 * q + 128], gains[:, 256 * q + 128:256 * q + 256]
                )
                total = gain * wide_values
                top, bottom = total[:half], total[half:]
                for k in range(2):
                    h = 2 * q + k
                    mask = low_lane if k == 0 else jnp.logical_not(low_lane)
                    own = jnp.where(mask, wide_values, 0.0).astype(jnp.bfloat16)
                    cumul_h = cumul[:, 128 * h:128 * h + 128]
                    row = u_rows[b, pl.ds(head0 + h, 1), :]
                    near = jnp.exp2(jnp.minimum(cumul_h - row[:, :half], 1.0))
                    near = (near * scores[score, :, :half]).astype(jnp.bfloat16)
                    far = jnp.exp2(jnp.minimum(cumul_h[half:] - row[:, half:], 1.0))
                    far = (far * scores[score, half:, half:]).astype(jnp.bfloat16)
                    near_sum = dot(near, own[:half])
                    top = top + near_sum[:half]
                    bottom = bottom + near_sum[half:] + dot(far, own[half:])
                base = pl.multiple_of(b * BLOCK, BLOCK)
                partial_out[pl.ds(base, half), at] = top
                partial_out[pl.ds(base + half, half), at] = bottom
                pair = slice(256 * q, 256 * q + 128), slice(256 * q + 128, 256 * q + 256)
                cumul_p = jnp.where(low_lane, cumul[:, pair[0]], cumul[:, pair[1]])
                log_p = jnp.where(low_lane, log_step[:, pair[0]], log_step[:, pair[1]])
                end = cumul_p[BLOCK - 1:BLOCK, :]
                grow[here, at] = jnp.exp2(cumul_p)
                update = (jnp.exp2(end - cumul_p + log_p) * wide_values).astype(jnp.bfloat16)
                fresh = dot(in_t[score], update)
                states[b + 1, :, at] = jnp.exp2(end) * states[b, :, at] + fresh
                befores[b + 1, :, at] = befores[b, :, at] + end
            return 0

        lax.fori_loop(0, blocks, one_block, 0)

    def carried_part(j):
        at = part_cols(j)
        group = (j * PART_HEADS) // GROUP_HEADS

        @pl.when(pos > 0)
        def _():
            state_copy(j).wait_recv()

        @pl.when(pos == 0)
        def _():
            arriving[:, at] = jnp.zeros((SSTATE, PART), jnp.bfloat16)

        @pl.when(pos < chain_len - 1)
        def _():
            before = arriving[:, at].astype(jnp.float32)
            after = jnp.exp2(befores[blocks, 0:1, at]) * before + states[blocks, :, at]
            leaving[:, at] = after.astype(jnp.bfloat16)
            state_copy(j).start()

        def one_block(b, _):
            here = block_rows(b)
            before = arriving[:, at].astype(jnp.float32)
            state = jnp.exp2(befores[b, 0:1, at]) * before + states[b, :, at]
            maps = out_map_buf[here, pl.ds(pl.multiple_of(group * SSTATE, SSTATE), SSTATE)]
            carried = dot(maps, state.astype(jnp.bfloat16)) * grow[here, at]
            out_buf[here, at] = (partial_out[here, at] + carried).astype(jnp.bfloat16)
            return 0

        lax.fori_loop(0, blocks, one_block, 0)
        for r in range(1, head_len):
            out_copy(j, r).start()
        out_own(j).start()

    def turn(i, _):
        @pl.when(i < parts)
        def _():
            local_part(i)

        @pl.when(jnp.logical_and(i >= pos, i < pos + parts))
        def _():
            carried_part(i - pos)

        return 0

    lax.fori_loop(0, parts + chain_len - 1, turn, 0)

    for i in range(3):
        for r in range(1, head_len):
            meta_copy(r, i).wait_send()

    def settle(j, _):
        for r in range(1, head_len):
            sig_copy(j, r).wait_send()
            out_copy(j, r).wait()
        out_own(j).wait()

        @pl.when(pos < chain_len - 1)
        def _():
            state_copy(j).wait_send()

        return 0

    lax.fori_loop(0, parts, settle, 0)


def shards(signal, input_map, output_map, step_size, decay_rate, skip_gain):
    head_len = lax.axis_size("head")
    chain_len = lax.axis_size("chain")
    rows = signal.shape[0]
    local_heads = HEADS // head_len
    cols = local_heads * CHANNEL_WIDTH
    parts = cols // PART
    groups = max(1, local_heads // GROUP_HEADS)
    all_rows = rows * head_len
    blocks = all_rows // BLOCK
    f32, bf16 = jnp.float32, jnp.bfloat16
    dma = pltpu.SemaphoreType.DMA
    anywhere = pl.BlockSpec(memory_space=pl.ANY)
    in_vmem = pl.BlockSpec(memory_space=pltpu.VMEM)
    return pl.pallas_call(
        functools.partial(kernel, head_len, chain_len),
        out_shape=jax.ShapeDtypeStruct(signal.shape, bf16),
        in_specs=[anywhere] * 4 + [in_vmem] * 2,
        out_specs=anywhere,
        scratch_shapes=[
            pltpu.VMEM((all_rows, cols), bf16),
            pltpu.VMEM((all_rows, groups * SSTATE), bf16),
            pltpu.VMEM((all_rows, groups * SSTATE), bf16),
            pltpu.VMEM((all_rows, HEADS), bf16),
            pltpu.VMEM((blocks, HEADS, BLOCK), f32),
            pltpu.VMEM((blocks * groups, BLOCK, BLOCK), f32),
            pltpu.VMEM((blocks * groups, SSTATE, BLOCK), bf16),
            pltpu.VMEM((HEADS, 128), f32),
            pltpu.VMEM((blocks + 1, SSTATE, cols), f32),
            pltpu.VMEM((blocks + 1, 8, cols), f32),
            pltpu.VMEM((all_rows, cols), f32),
            pltpu.VMEM((all_rows, cols), f32),
            pltpu.VMEM((all_rows, cols), bf16),
            pltpu.VMEM((SSTATE, cols), bf16),
            pltpu.VMEM((SSTATE, cols), bf16),
            dma((3,)), dma((3, head_len)), dma((3, head_len)),
            dma, dma((parts, head_len)), dma((parts, head_len)),
            dma((parts,)), dma((parts,)),
            dma((parts,)), dma((parts, head_len)), dma((parts, head_len)),
        ],
        compiler_params=pltpu.CompilerParams(
            collective_id=0, has_side_effects=True, vmem_limit_bytes=60 * 1024 * 1024
        ),
    )(signal, input_map, output_map, step_size, decay_rate[None, :], skip_gain[None, :])


def solution(mesh):
    return jax.shard_map(
        shards,
        mesh=mesh,
        in_specs=(
            P(("chain", "head"), None),
            P(("chain", "head"), None),
            P(("chain", "head"), None),
            P(("chain", "head"), None),
            P(),
            P(),
        ),
        out_specs=P(("chain", "head"), None),
        check_vma=False,
    )
```
